32 devices in a mesh: lon: 16 (over z, y, core), lat: 2 (over x).
Axes of the slice: x: 2, y: 2, z: 4, core: 2. Of those that a mesh axis runs over, the one named last changes fastest.
Arguments:
- state: bfloat16 [64, 192, 256], P(('lon', 'lat')), may hold values from -6 to 6
- cotangent: bfloat16 [64, 192, 256], P(('lon', 'lat')), may hold values from -6 to 6
- land_mask: int32 [64, 256], P(('lon', 'lat')), may hold values from 0 to 1, as said below
- neighbour_codes: int32 [64, 8], P(('lon', 'lat')), may hold values from -1 to 127, as said below
- conv_weight: float32 [2, 49, 192], replicated, may hold values from -0.875 to 0.875
- conv_bias: float32 [2, 192], replicated, may hold values from -3 to 3
- normalizer_multiplier: float32 [2, 192], replicated, may hold values from 0.25 to 1.75
- norm_bias: float32 [2, 192], replicated, may hold values from -3 to 3
- expand_weight: bfloat16 [2, 192, 640], replicated, may hold values from -0.4375 to 0.4375
- expand_bias: float32 [2, 640], replicated, may hold values from -3 to 3
- project_weight: bfloat16 [2, 640, 192], replicated, may hold values from -0.25 to 0.25
- project_bias: float32 [2, 192], replicated, may hold values from -3 to 3
- layer_scale: float32 [2, 192], replicated, may hold values from 0.3 to 1
Outputs:
- predicted_field: bfloat16 [64, 192, 256], P(('lon', 'lat'))
- state_gradient: bfloat16 [64, 192, 256], P(('lon', 'lat'))
- conv_weight_grad: float32 [2, 49, 192], replicated
- perchannel_sensitivities: float32 [2, 5, 192], replicated
- expand_weight_grad: float32 [2, 192, 640], replicated
- expand_bias_grad: float32 [2, 640], replicated
- project_weight_grad: float32 [2, 640, 192], replicated
The draws below stay inside these ranges and needn't reach their ends.
Inputs may be any that keep to these rules, and one draw needn't show every extreme that they name: `neighbour_codes`: slots are numbered device after device, lon index slowest, 2 a device. The device at lon index a and lat index b holds in its first slots, west to east, the ocean tiles among tile columns 2 a to 2 a + 1 of tile row b; its other slots are empty and hold -1 in every direction. The code is -1 where the neighbour is land or lies south of row 0. Tile columns are cyclic. North of the top row lies the fold: tile column c beyond the top is tile column 31 - c of the top row, turned half round, and such codes carry + 64. Links are mutual. `land_mask`: every cell of an empty slot is 0.
All inputs are finite; a program needn't handle non-finite values.
Results may differ from the reference program's by a relative error of at most 0.008.
Values may be sent and summed in bfloat16 or wider, within the bound.
A program may use at most 128 MiB of HBM per device.

```python
import math
import jax
import jax.numpy as jnp
from jax import lax

C = 192
HID = 640
TS = 16
SLOTS = 2
NB = 2
CELLS = 256
TILES = 64
N_LON = 16
N_LAT = 2


DIRECTIONS = ((0, 1), (0, -1), (-1, 0), (1, 0), (-1, 1), (1, 1), (-1, -1), (1, -1))


def ocean_layout(key):
    columns = SLOTS * N_LON
    draws = jax.random.randint(jax.random.fold_in(key, 5), (columns, N_LAT), 0, 10)
    block = jnp.arange(columns) // SLOTS
    forced = (block == 0) | (block == N_LON - 1)
    ocean = (draws < 7) | forced[:, None]
    wet_count = ocean.astype(jnp.int32).reshape(N_LON, SLOTS, N_LAT)
    ranking = jnp.cumsum(wet_count, axis=1) - wet_count
    matched = (wet_count[:, :, :, None] == 1) & (ranking[:, :, :, None] == jnp.arange(SLOTS)[None, None, None, :])
    living = jnp.any(matched, axis=1)
    within = jnp.sum(jnp.where(matched, jnp.arange(SLOTS)[None, :, None, None], 0), axis=1)
    column_of = within + SLOTS * jnp.arange(N_LON)[:, None, None]
    devices = jnp.arange(N_LON)[:, None, None] * N_LAT + jnp.arange(N_LAT)[None, None, :]
    tile_at = (devices * SLOTS + ranking).reshape(columns, N_LAT)
    return (ocean, living, column_of, tile_at)


def draw_neighbour_codes(key, part):
    ocean, living, column_of, tile_at = ocean_layout(key)
    columns = SLOTS * N_LON
    tile_total = columns * N_LAT
    row_of = jnp.broadcast_to(jnp.arange(N_LAT)[None, :, None], column_of.shape)
    collected = []
    for step_x, step_y in DIRECTIONS:
        target_row = row_of + step_y
        beyond = target_row > N_LAT - 1
        target_col = jnp.where(beyond, columns - 1 - (column_of + step_x), column_of + step_x) % columns
        safe_row = jnp.clip(target_row, 0, N_LAT - 1)
        found = ocean[target_col, safe_row] & (target_row >= 0) & living
        linked_code = tile_at[target_col, safe_row] + tile_total * beyond.astype(jnp.int32)
        collected.append(jnp.where(found, linked_code, -1))
    return jnp.stack(collected, axis=-1).reshape(tile_total, 8).astype(jnp.int32)


def draw_land_mask(key, part):
    ocean, living, column_of, tile_at = ocean_layout(key)
    tile_total = SLOTS * N_LON * N_LAT
    cell_draws = jax.random.randint(jax.random.fold_in(key, 11), (tile_total, TS * TS), 0, 20)
    levels = jax.random.randint(jax.random.fold_in(key, 12), (tile_total, 1), 12, 20)
    wet_cells = (cell_draws < levels) & living.reshape(tile_total, 1)
    return wet_cells.astype(jnp.int32)


def block_scale(key, dims, cuts, low, largest):
    def one(dim, blocks):
        heights = jax.random.uniform(jax.random.fold_in(jax.random.fold_in(key, 6), dim), (blocks,), jnp.float32, low / len(cuts), largest / len(cuts))
        return jnp.repeat(jnp.exp(heights), dims[dim] // blocks).reshape((-1,) + (1,) * (len(dims) - dim - 1))

    loudness = one(*cuts[0])
    for cut in cuts[1:]:
        loudness = loudness * one(*cut)
    return loudness


def scatter_about(key, shape, scale, reach, split=(), kind=jnp.bfloat16):
    entries = jax.random.normal(key, shape, jnp.float32) * scale
    if len(split) > 0:
        entries = block_scale(key, shape, split, -0.22, 0.18) * entries
    return jnp.clip(entries, min=-reach, max=reach).astype(kind)


def setup_inputs(seed: int = 0) -> dict:
    seeds = jax.random.split(jax.random.key(seed), 14)
    state = scatter_about(seeds[0], (TILES, C, CELLS), 1.0, 6.0, ((0, 32),))
    cotangent = scatter_about(seeds[1], (TILES, C, CELLS), 1.0, 6.0, ((0, 32),))
    land_mask = draw_land_mask(jax.random.fold_in(seeds[13], 71), 0)
    neighbour_codes = draw_neighbour_codes(jax.random.fold_in(seeds[13], 71), 0)
    conv_weight = scatter_about(seeds[4], (NB, 49, C), 49 ** -0.5, 0.875, (), jnp.float32)
    conv_bias = scatter_about(seeds[5], (NB, C), 0.5, 3.0, (), jnp.float32)
    normalizer_multiplier = jnp.clip(1.0 + 0.15 * jax.random.normal(seeds[6], (NB, C), jnp.float32), 0.25, 1.75)
    norm_bias = scatter_about(seeds[7], (NB, C), 0.5, 3.0, (), jnp.float32)
    expand_weight = scatter_about(seeds[8], (NB, C, HID), C ** -0.5, 0.4375)
    expand_bias = scatter_about(seeds[9], (NB, HID), 0.5, 3.0, (), jnp.float32)
    project_weight = scatter_about(seeds[10], (NB, HID, C), HID ** -0.5, 0.25)
    project_bias = scatter_about(seeds[11], (NB, C), 0.5, 3.0, (), jnp.float32)
    layer_scale = jnp.clip(jax.random.uniform(seeds[12], (NB, C), jnp.float32, 0.3, 1.0), 0.3, 1.0)
    return {"state": state, "cotangent": cotangent, "land_mask": land_mask, "neighbour_codes": neighbour_codes, "conv_weight": conv_weight, "conv_bias": conv_bias, "normalizer_multiplier": normalizer_multiplier, "norm_bias": norm_bias, "expand_weight": expand_weight, "expand_bias": expand_bias, "project_weight": project_weight, "project_bias": project_bias, "layer_scale": layer_scale}


SIDE_OPPOSITE = (1, 0, 3, 2)
CORNER_OPPOSITE = (3, 2, 1, 0)
GELU_SCALE = 0.7978845608028654
GELU_CUBIC = 0.044715

def gelu_value(values):
    inner = GELU_SCALE * (values + GELU_CUBIC * values * values * values)
    return 0.5 * values * (1.0 + jnp.tanh(inner))

def gelu_slope(values):
    tangent = jnp.tanh(GELU_SCALE * (values + GELU_CUBIC * values * values * values))
    return 0.5 * (1.0 + tangent) + 0.5 * values * (1.0 - tangent * tangent) * GELU_SCALE * (1.0 + 3.0 * GELU_CUBIC * values * values)

def cut_pieces(square, inner_low, inner_high):
    extent = square.shape[-1]
    leading = square.shape[:-2]
    side_parts = (square[..., extent - 3:, inner_low:inner_high], square[..., :3, inner_low:inner_high], square[..., inner_low:inner_high, :3], square[..., inner_low:inner_high, extent - 3:])
    corner_parts = (square[..., extent - 3:, :3], square[..., extent - 3:, extent - 3:], square[..., :3, :3], square[..., :3, extent - 3:])
    side_pieces = jnp.concatenate([section.reshape(leading + (-1,)) for section in side_parts], axis=-1)
    corner_pieces = jnp.concatenate([section.reshape(leading + (-1,)) for section in corner_parts], axis=-1)
    return (side_pieces, corner_pieces)

def linked_pieces(side_pool, corner_pool, pool_rows, flipped):
    segment = side_pool.shape[-1] // 4
    linked = []
    for which in range(4):
        fetched = side_pool[pool_rows[:, which]]
        rotated = jnp.flip(fetched[..., which * segment:(which + 1) * segment], axis=-1)
        opposite = SIDE_OPPOSITE[which]
        facing = fetched[..., opposite * segment:(opposite + 1) * segment]
        linked.append(jnp.where(flipped[:, which][:, None, None], rotated, facing))
    for which in range(4):
        fetched = corner_pool[pool_rows[:, 4 + which]]
        rotated = jnp.flip(fetched[..., which * 9:(which + 1) * 9], axis=-1)
        opposite = CORNER_OPPOSITE[which]
        facing = fetched[..., opposite * 9:(opposite + 1) * 9]
        linked.append(jnp.where(flipped[:, 4 + which][:, None, None], rotated, facing))
    return linked

def assemble(tile_grid, linked):
    tile_count, channels, extent = (tile_grid.shape[0], tile_grid.shape[1], tile_grid.shape[2])
    north_band = linked[0].reshape(tile_count, channels, 3, extent)
    south_band = linked[1].reshape(tile_count, channels, 3, extent)
    west_band = linked[2].reshape(tile_count, channels, extent, 3)
    east_band = linked[3].reshape(tile_count, channels, extent, 3)
    corners = [section.reshape(tile_count, channels, 3, 3) for section in linked[4:]]
    bottom = jnp.concatenate([corners[2], south_band, corners[3]], axis=-1)
    middle = jnp.concatenate([west_band, tile_grid, east_band], axis=-1)
    top_band = jnp.concatenate([corners[0], north_band, corners[1]], axis=-1)
    return jnp.concatenate([bottom, middle, top_band], axis=-2)

def add_border(gradient, linked):
    tile_count, channels, extent = (gradient.shape[0], gradient.shape[1], gradient.shape[2])
    side_shape = (tile_count, channels, 3, extent)
    column_shape = (tile_count, channels, extent, 3)
    corner_shape = (tile_count, channels, 3, 3)
    gradient = gradient.at[:, :, extent - 3:, :].add(linked[0].reshape(side_shape).astype(jnp.float32))
    gradient = gradient.at[:, :, :3, :].add(linked[1].reshape(side_shape).astype(jnp.float32))
    gradient = gradient.at[:, :, :, :3].add(linked[2].reshape(column_shape).astype(jnp.float32))
    gradient = gradient.at[:, :, :, extent - 3:].add(linked[3].reshape(column_shape).astype(jnp.float32))
    gradient = gradient.at[:, :, extent - 3:, :3].add(linked[4].reshape(corner_shape).astype(jnp.float32))
    gradient = gradient.at[:, :, extent - 3:, extent - 3:].add(linked[5].reshape(corner_shape).astype(jnp.float32))
    gradient = gradient.at[:, :, :3, :3].add(linked[6].reshape(corner_shape).astype(jnp.float32))
    gradient = gradient.at[:, :, :3, extent - 3:].add(linked[7].reshape(corner_shape).astype(jnp.float32))
    return gradient

def depthwise(padded, kernel, extent):
    broadened_hidden = padded.astype(jnp.float32)
    summed = jnp.zeros(padded.shape[:2] + (extent, extent), jnp.float32)
    for upward in range(7):
        for across in range(7):
            summed = summed + kernel[7 * upward + across][None, :, None, None] * broadened_hidden[:, :, upward:upward + extent, across:across + extent]
    return summed

def depthwise_adjoint(gradient, kernel, extent):
    spread = jnp.pad(gradient, ((0, 0), (0, 0), (6, 6), (6, 6)))
    summed = jnp.zeros(gradient.shape[:2] + (extent + 6, extent + 6), jnp.float32)
    for upward in range(7):
        for across in range(7):
            summed = summed + kernel[7 * upward + across][None, :, None, None] * spread[:, :, 6 - upward:12 - upward + extent, 6 - across:12 - across + extent]
    return summed

def forward_block(padded, land_part, weights):
    kernel, conv_shift, gain, norm_shift, expand_mat, expand_shift, project_mat, project_shift, scale_row = weights
    tile_count, channels, extent = (padded.shape[0], padded.shape[1], padded.shape[2] - 6)
    conv = depthwise(padded, kernel, extent) + conv_shift[None, :, None, None]
    flat = conv.reshape(tile_count, channels, extent * extent)
    average = lax.optimization_barrier(jnp.mean(flat, axis=1, keepdims=True))
    centred_values = flat - average
    inverse = lax.rsqrt(lax.optimization_barrier(jnp.mean(centred_values * centred_values, axis=1, keepdims=True)) + 1e-06)
    unit = centred_values * inverse
    normed = (unit * gain[None, :, None] + norm_shift[None, :, None]).astype(jnp.bfloat16)
    preact = jnp.einsum('ch,scp->shp', expand_mat.astype(jnp.float32), normed.astype(jnp.float32)) + expand_shift[None, :, None]
    hidden = gelu_value(preact).astype(jnp.bfloat16)
    branch = jnp.einsum('hc,shp->scp', project_mat.astype(jnp.float32), hidden.astype(jnp.float32)) + project_shift[None, :, None]
    centre_cells = padded[:, :, 3:extent + 3, 3:extent + 3].reshape(tile_count, channels, extent * extent).astype(jnp.float32)
    ocean_cells = land_part.astype(jnp.float32)[:, None, :]
    result = (ocean_cells * (centre_cells + scale_row[None, :, None] * branch)).astype(jnp.bfloat16)
    return (result, (unit, inverse, normed, preact, hidden, branch))

def backward_block(padded, land_part, weights, saved, arriving_sensitivity):
    kernel, conv_shift, gain, norm_shift, expand_mat, expand_shift, project_mat, project_shift, scale_row = weights
    unit, inverse, normed, preact, hidden, branch = saved
    tile_count, channels, extent = (padded.shape[0], padded.shape[1], padded.shape[2] - 6)
    ocean_cells = land_part.astype(jnp.float32)[:, None, :]
    masked = ocean_cells * arriving_sensitivity.astype(jnp.float32)
    branch_grad = scale_row[None, :, None] * masked
    branch_low = branch_grad.astype(jnp.bfloat16)
    hidden_grad = jnp.einsum('hc,scp->shp', project_mat.astype(jnp.float32), branch_low.astype(jnp.float32))
    preact_grad = hidden_grad * gelu_slope(preact)
    preact_low = preact_grad.astype(jnp.bfloat16)
    normed_grad = jnp.einsum('ch,shp->scp', expand_mat.astype(jnp.float32), preact_low.astype(jnp.float32))
    unit_grad = normed_grad * gain[None, :, None]
    conv_grad = inverse * (unit_grad - lax.optimization_barrier(jnp.mean(unit_grad, axis=1, keepdims=True)) - unit * lax.optimization_barrier(jnp.mean(unit_grad * unit, axis=1, keepdims=True)))
    convolution_reduced = conv_grad.astype(jnp.bfloat16)
    grad_grid = convolution_reduced.reshape(tile_count, channels, extent, extent).astype(jnp.float32)
    adjoint = depthwise_adjoint(grad_grid, kernel, extent)
    broadened_hidden = padded.astype(jnp.float32)
    kernel_grad = jnp.stack([lax.optimization_barrier(jnp.sum(grad_grid * broadened_hidden[:, :, upward:upward + extent, across:across + extent], axis=(0, 2, 3))) for upward in range(7) for across in range(7)])
    channel_grad = jnp.stack([lax.optimization_barrier(jnp.sum(conv_grad, axis=(0, 2))), lax.optimization_barrier(jnp.sum(normed_grad * unit, axis=(0, 2))), lax.optimization_barrier(jnp.sum(normed_grad, axis=(0, 2))), lax.optimization_barrier(jnp.sum(branch_grad, axis=(0, 2))), lax.optimization_barrier(jnp.sum(masked * branch, axis=(0, 2)))])
    expand_grad = jnp.einsum('scp,shp->ch', normed.astype(jnp.float32), preact_low.astype(jnp.float32))
    expand_shift_grad = lax.optimization_barrier(jnp.sum(preact_grad, axis=(0, 2)))
    project_grad = jnp.einsum('shp,scp->hc', hidden.astype(jnp.float32), branch_low.astype(jnp.float32))
    local_grad = masked.reshape(tile_count, channels, extent, extent) + adjoint[:, :, 3:extent + 3, 3:extent + 3]
    side_sent, corner_sent = cut_pieces(adjoint, 3, extent + 3)
    return (local_grad, side_sent.astype(jnp.bfloat16), corner_sent.astype(jnp.bfloat16), (kernel_grad, channel_grad, expand_grad, expand_shift_grad, project_grad))

def with_blank(pieces_all):
    return jnp.concatenate([pieces_all, jnp.zeros((1,) + pieces_all.shape[1:], pieces_all.dtype)], axis=0)

def reference(state, cotangent, land_mask, neighbour_codes, conv_weight, conv_bias, normalizer_multiplier, norm_bias, expand_weight, expand_bias, project_weight, project_bias, layer_scale):
    flipped = neighbour_codes >= TILES
    pool_rows = jnp.where(neighbour_codes < 0, TILES, neighbour_codes % TILES).astype(jnp.int32)
    batch = 4 * SLOTS
    rounds = TILES // batch
    scale_factor = 1.0 / math.sqrt(TILES * CELLS)
    masks = land_mask.reshape(rounds, batch, CELLS)

    def weights_of(layer):
        return (conv_weight[layer], conv_bias[layer], normalizer_multiplier[layer], norm_bias[layer], expand_weight[layer], expand_bias[layer], project_weight[layer], project_bias[layer], layer_scale[layer])

    def padded_of(values):
        tile_grid = values.reshape(TILES, C, TS, TS)
        side_pieces, corner_pieces = cut_pieces(tile_grid, 0, TS)
        linked = linked_pieces(with_blank(side_pieces), with_blank(corner_pieces), pool_rows, flipped)
        return assemble(tile_grid, linked)
    current_field = state
    padded_list = []
    for layer in range(NB):
        weights = weights_of(layer)
        padded = padded_of(current_field)
        padded_list.append(padded)

        def forward_round(inputs, weights=weights):
            return forward_block(inputs[0], inputs[1], weights)[0]
        current_field = lax.map(forward_round, (padded.reshape(rounds, batch, C, TS + 6, TS + 6), masks)).reshape(TILES, C, CELLS)
    predicted_field = current_field
    arriving_sensitivity = cotangent
    gradients = [None] * NB
    for layer in reversed(range(NB)):
        weights = weights_of(layer)

        def backward_round(inputs, weights=weights):
            padded_part, mask_part, upstream_part = inputs
            result, saved = forward_block(padded_part, mask_part, weights)
            return backward_block(padded_part, mask_part, weights, saved, upstream_part)
        local_grad, side_sent, corner_sent, partial_grads = lax.map(backward_round, (padded_list[layer].reshape(rounds, batch, C, TS + 6, TS + 6), masks, arriving_sensitivity.reshape(rounds, batch, C, CELLS)))
        local_grad = local_grad.reshape(TILES, C, TS, TS)
        side_sent = side_sent.reshape(TILES, C, -1)
        corner_sent = corner_sent.reshape(TILES, C, -1)
        linked = linked_pieces(with_blank(side_sent), with_blank(corner_sent), pool_rows, flipped)
        arriving_sensitivity = add_border(local_grad, linked).reshape(TILES, C, CELLS).astype(jnp.bfloat16)
        gradients[layer] = tuple((lax.optimization_barrier(jnp.sum(member, axis=0)) * scale_factor for member in partial_grads))
    batched_patches = [jnp.stack([gradients[layer][member] for layer in range(NB)]) for member in range(5)]
    return (predicted_field, arriving_sensitivity, batched_patches[0], batched_patches[1], batched_patches[2], batched_patches[3], batched_patches[4])
```

```python
import functools
import math

import jax
import jax.numpy as jnp
from jax import lax
from jax.experimental import pallas as pl
from jax.experimental.pallas import tpu as pltpu
from jax.sharding import PartitionSpec as P

MESH = pl.DeviceIdType.MESH
GELU_SCALE = 0.7978845608028654
GELU_CUBIC = 0.044715
VMEM_LIMIT = 50 * 1024 * 1024
F32 = jnp.float32
BF16 = jnp.bfloat16


def exchange_kernel(lon_count, lat_count, rows_ref, cols_ref, got_rows, got_cols, send_sem, recv_sem):
    a = lax.axis_index("lon")
    b = lax.axis_index("lat")
    top = b == lat_count - 1
    bottom = b == 0

    def wrapped(i):
        return lax.rem(i + 2 * lon_count, lon_count)

    def across(d):
        return wrapped(lon_count - 1 - a - d)

    west, east = wrapped(a - 1), wrapped(a + 1)
    barrier = pltpu.get_barrier_semaphore()

    def greet(lon, lat):
        pl.semaphore_signal(barrier, inc=1, device_id=(lon, lat), device_id_type=MESH)

    greet(west, b)
    greet(east, b)
    for d in (-1, 0, 1):

        @pl.when(jnp.logical_not(top))
        def _():
            greet(wrapped(a + d), b + 1)

        @pl.when(jnp.logical_and(top, across(d) != a))
        def _():
            greet(across(d), b)

        @pl.when(jnp.logical_not(bottom))
        def _():
            greet(wrapped(a + d), b - 1)

    peers = 2 + jnp.where(bottom, 0, 3)
    for d in (-1, 0, 1):
        peers = peers + jnp.where(jnp.logical_and(top, across(d) == a), 0, 1)
    pl.semaphore_wait(barrier, peers)

    def message(source, landing, number, sending, lon, lat):
        return pltpu.make_async_remote_copy(
            src_ref=source,
            dst_ref=landing,
            send_sem=send_sem.at[sending],
            recv_sem=recv_sem.at[number],
            device_id=(lon, lat),
            device_id_type=MESH,
        )

    def north(d):
        return message(rows_ref.at[0], got_rows.at[4 - d], 4 - d, 1 + d, wrapped(a + d), b + 1)

    def fold(d):
        return message(rows_ref.at[0], got_rows.at[1 + d], 1 + d, 1 + d, across(d), b)

    def own(d):
        return pltpu.make_async_copy(rows_ref.at[0], got_rows.at[1 + d], recv_sem.at[1 + d])

    def south(d):
        return message(rows_ref.at[1], got_rows.at[1 - d], 1 - d, 4 + d, wrapped(a + d), b - 1)

    def to_west():
        return message(cols_ref.at[0], got_cols.at[1], 7, 6, west, b)

    def to_east():
        return message(cols_ref.at[1], got_cols.at[0], 6, 7, east, b)

    for d in (0, -1, 1):

        @pl.when(jnp.logical_not(top))
        def _():
            north(d).start()

        @pl.when(jnp.logical_and(top, across(d) != a))
        def _():
            fold(d).start()

        @pl.when(jnp.logical_and(top, across(d) == a))
        def _():
            own(d).start()

        @pl.when(jnp.logical_not(bottom))
        def _():
            south(d).start()

    to_west().start()
    to_east().start()
    for d in (0, -1, 1):

        @pl.when(jnp.logical_not(top))
        def _():
            north(d).wait_send()
            message(rows_ref.at[1], got_rows.at[1 + d], 1 + d, 4 - d, wrapped(a + d), b + 1).wait_recv()

        @pl.when(jnp.logical_and(top, across(d) != a))
        def _():
            fold(d).wait_send()
            fold(d).wait_recv()

        @pl.when(jnp.logical_and(top, across(d) == a))
        def _():
            own(d).wait()

        @pl.when(jnp.logical_not(bottom))
        def _():
            south(d).wait_send()
            message(rows_ref.at[0], got_rows.at[4 + d], 4 + d, 1 - d, wrapped(a + d), b - 1).wait_recv()

    to_west().wait_send()
    to_east().wait_send()
    to_west().wait_recv()
    to_east().wait_recv()


def exchange(rows, cols, identity):
    lon_count, lat_count = lax.axis_size("lon"), lax.axis_size("lat")
    vmem = pl.BlockSpec(memory_space=pltpu.VMEM)
    return pl.pallas_call(
        functools.partial(exchange_kernel, lon_count, lat_count),
        out_shape=(
            jax.ShapeDtypeStruct((6,) + rows.shape[1:], rows.dtype),
            jax.ShapeDtypeStruct((2,) + cols.shape[1:], cols.dtype),
        ),
        in_specs=[vmem, vmem],
        out_specs=(vmem, vmem),
        scratch_shapes=[pltpu.SemaphoreType.DMA((8,)), pltpu.SemaphoreType.DMA((8,))],
        compiler_params=pltpu.CompilerParams(
            collective_id=identity, has_side_effects=True, vmem_limit_bytes=VMEM_LIMIT
        ),
    )(rows, cols)


def link_table(codes, slots):
    lon_count, lat_count = lax.axis_size("lon"), lax.axis_size("lat")
    total = slots * lon_count * lat_count
    here = lax.axis_index("lon")
    flipped = codes >= total
    target = jnp.where(flipped, codes - total, codes)
    lon_there = target // slots // lat_count
    centre = jnp.where(flipped, lon_count - 1 - here, here)
    return codes >= 0, lon_there != centre, target % slots


def linked_strips(got_rows, got_cols, own_cols, table, width):
    valid, away, slot = table
    slots = got_rows.shape[1]

    def spread(flags, rank):
        return flags.reshape((-1,) + (1,) * (rank - 1))

    def pick(near, far, e, low, high):
        result = jnp.zeros((slots,) + near.shape[1:2] + (high - low,) + near.shape[3:], near.dtype)
        for s in range(slots):
            for pool, wanted in ((near, False), (far, True)):
                if pool is None:
                    continue
                hit = valid[:, e] & (slot[:, e] == s)
                if far is not None:
                    hit = hit & (away[:, e] == wanted)
                result = jnp.where(spread(hit, 4), pool[s][None, :, low:high], result)
        return result

    extent = got_cols.shape[3]
    edge = (width - extent) // 2
    north = pick(got_rows[1], None, 0, edge, width - edge)
    south = pick(got_rows[4], None, 1, edge, width - edge)
    west = pick(own_cols[1], got_cols[0], 2, 0, extent)
    east = pick(own_cols[0], got_cols[1], 3, 0, extent)
    north_west = pick(got_rows[1], got_rows[0], 4, width - 3, width)
    north_east = pick(got_rows[1], got_rows[2], 5, 0, 3)
    south_west = pick(got_rows[4], got_rows[3], 6, width - 3, width)
    south_east = pick(got_rows[4], got_rows[5], 7, 0, 3)
    west = west.transpose(0, 2, 1, 3)
    east = east.transpose(0, 2, 1, 3)
    return north, south, west, east, north_west, north_east, south_west, south_east


def padded_of(x, table, identity):
    extent = x.shape[1]
    top = lax.axis_index("lat") == lax.axis_size("lat") - 1
    north, south = x[:, extent - 3 :], x[:, :3]
    north = jnp.where(top, jnp.flip(north, (1, 2)), north)
    cols = jnp.stack([x[:, :, :3].transpose(0, 2, 1, 3), x[:, :, extent - 3 :].transpose(0, 2, 1, 3)])
    got_rows, got_cols = exchange(jnp.stack([north, south]), cols, identity)
    n, s, w, e, nw, ne, sw, se = linked_strips(got_rows, got_cols, cols, table, extent)
    padded = jnp.concatenate(
        [
            jnp.concatenate([sw, s, se], axis=2),
            jnp.concatenate([w, x, e], axis=2),
            jnp.concatenate([nw, n, ne], axis=2),
        ],
        axis=1,
    )
    return jnp.pad(padded.astype(F32), ((0, 0), (0, 0), (0, 2), (0, 0)))


def gradient_of(local, adjoint, table, identity):
    extent = local.shape[1]
    side = extent + 6
    top = lax.axis_index("lat") == lax.axis_size("lat") - 1
    sent = adjoint[:, :, :side].astype(BF16)
    north, south = sent[:, side - 3 :], sent[:, :3]
    north = jnp.where(top, jnp.flip(north, (1, 2)), north)
    rows = jnp.pad(jnp.stack([north, south]), ((0, 0), (0, 0), (0, 0), (0, -side % 16), (0, 0)))
    middle = sent[:, 3 : extent + 3]
    cols = jnp.stack(
        [middle[:, :, :3].transpose(0, 2, 1, 3), middle[:, :, side - 3 :].transpose(0, 2, 1, 3)]
    )
    got_rows, got_cols = exchange(rows, cols, identity)
    n, s, w, e, nw, ne, sw, se = linked_strips(got_rows, got_cols, cols, table, side)
    rest = extent - 3

    def placed(piece, row, col):
        row = (0, rest) if row == 0 else (rest, 0)
        if piece.shape[1] == extent:
            row = (0, 0)
        col = (0, rest) if col == 0 else (rest, 0)
        if piece.shape[2] == extent:
            col = (0, 0)
        return jnp.pad(piece.astype(F32), ((0, 0), row, col, (0, 0)))

    return (
        local
        + placed(n, 1, 0)
        + placed(s, 0, 0)
        + placed(w, 0, 0)
        + placed(e, 0, 1)
        + placed(nw, 1, 0)
        + placed(ne, 1, 1)
        + placed(sw, 0, 0)
        + placed(se, 0, 1)
    ).astype(BF16)


def block_kernel(with_forward, with_backward, padded_ref, mask_ref, *refs):
    refs = list(refs)
    x_ref = refs.pop(0) if with_forward else None
    saved_ref = None if with_forward else refs.pop(0)
    g_ref = refs.pop(0) if with_backward else None
    kernel_ref, cb_ref, gain_ref, shift_ref, we_ref, eb_ref, wp_ref, pb_ref, scale_ref = refs[:9]
    refs = refs[9:]
    out_ref = refs.pop(0) if with_forward else None
    conv_ref = refs.pop(0) if with_forward else saved_ref
    if with_backward:
        local_ref, adj_ref, kg_ref, pc_ref, eg_ref, ebg_ref, pg_ref = refs[:7]
        refs = refs[7:]
    shifted = refs.pop(0)
    tiles, padded_side, _, channels = padded_ref.shape
    extent = padded_side - 6
    cells = extent * extent
    count = tiles * cells

    for v in range(7):
        for t in range(tiles):
            shifted[v, t] = padded_ref[t, :, v : v + extent, :]

    if with_forward:
        step = 4
        for t in range(tiles):

            def conv_rows(i, carry, t=t):
                low = i * step
                total = jnp.zeros((step, extent, channels), F32)
                for u in range(7):
                    for v in range(7):
                        total = total + kernel_ref[7 * u + v : 7 * u + v + 1, :][None] * (
                            shifted[v, t, pl.ds(low + u, step)]
                        )
                total = total + cb_ref[...][None]
                start = pl.multiple_of(t * cells + low * extent, step * extent)
                conv_ref[pl.ds(start, step * extent), :] = total.reshape(step * extent, channels)
                return carry

            lax.fori_loop(0, extent // step, conv_rows, 0)

    conv = conv_ref[...]
    centred = conv - jnp.mean(conv, axis=1, keepdims=True)
    inverse = lax.rsqrt(jnp.mean(centred * centred, axis=1, keepdims=True) + 1e-06)
    unit = centred * inverse
    normed = (unit * gain_ref[...] + shift_ref[...]).astype(BF16)
    preact = jnp.dot(normed, we_ref[...], preferred_element_type=F32) + eb_ref[...]
    tangent = jnp.tanh(GELU_SCALE * (preact + GELU_CUBIC * preact * preact * preact))
    hidden = (0.5 * preact * (1.0 + tangent)).astype(BF16)
    branch = jnp.dot(hidden, wp_ref[...], preferred_element_type=F32) + pb_ref[...]
    mask = mask_ref[...]
    if with_forward:
        out_ref[...] = (mask * (x_ref[...].astype(F32) + scale_ref[...] * branch)).astype(BF16)
    if not with_backward:
        return

    grad, low_grad = refs
    factor = scale_of(count)
    masked = mask * g_ref[...].astype(F32)
    branch_grad = scale_ref[...] * masked
    branch_low = branch_grad.astype(BF16)
    hidden_grad = lax.dot_general(
        branch_low, wp_ref[...], (((1,), (1,)), ((), ())), preferred_element_type=F32
    )
    slope = 0.5 * (1.0 + tangent) + 0.5 * preact * (1.0 - tangent * tangent) * GELU_SCALE * (
        1.0 + 3.0 * GELU_CUBIC * preact * preact
    )
    preact_grad = hidden_grad * slope
    preact_low = preact_grad.astype(BF16)
    normed_grad = lax.dot_general(
        preact_low, we_ref[...], (((1,), (1,)), ((), ())), preferred_element_type=F32
    )
    w = normed_grad * gain_ref[...]
    conv_grad = inverse * (
        w
        - jnp.mean(w, axis=1, keepdims=True)
        - unit * jnp.mean(w * unit, axis=1, keepdims=True)
    )

    def row_sum(values):
        return factor * jnp.sum(values, axis=0, keepdims=True)

    pc_ref[0:1, :] = row_sum(conv_grad)
    pc_ref[1:2, :] = row_sum(normed_grad * unit)
    pc_ref[2:3, :] = row_sum(normed_grad)
    pc_ref[3:4, :] = row_sum(branch_grad)
    pc_ref[4:5, :] = row_sum(masked * branch)
    ebg_ref[...] = row_sum(preact_grad)
    eg_ref[...] = factor * lax.dot_general(
        normed, preact_low, (((0,), (0,)), ((), ())), preferred_element_type=F32
    )
    pg_ref[...] = factor * lax.dot_general(
        hidden, branch_low, (((0,), (0,)), ((), ())), preferred_element_type=F32
    )
    grid = conv_grad.astype(BF16).astype(F32).reshape(tiles, extent, extent, channels)

    grad[...] = jnp.zeros_like(grad)
    for t in range(tiles):
        grad[t, 6 : 6 + extent, 8 : 8 + extent, :] = grid[t]

    for v in range(7):
        sums = tuple(jnp.zeros((extent, channels), F32) for _ in range(7))
        for t in range(tiles):

            def one_row(r, sums, t=t, v=v):
                row = grad[t, 6 + r, 8 : 8 + extent, :]
                return tuple(sums[u] + row * shifted[v, t, r + u] for u in range(7))

            sums = lax.fori_loop(0, extent, one_row, sums)
        for u in range(7):
            kg_ref[7 * u + v : 7 * u + v + 1, :] = row_sum(sums[u])

    wide = adj_ref.shape[2]
    for t in range(tiles):
        for v in range(7):
            low_grad[v] = grad[t, :, 8 - v : 8 - v + wide, :]

        def adjoint_rows(i, carry, t=t):
            low = i * 2
            total = jnp.zeros((2, wide, channels), F32)
            for u in range(7):
                for v in range(7):
                    total = total + kernel_ref[7 * u + v : 7 * u + v + 1, :][None] * (
                        low_grad[v, pl.ds(low + 6 - u, 2)]
                    )
            adj_ref[t, pl.ds(low, 2)] = total
            return carry

        lax.fori_loop(0, padded_side // 2, adjoint_rows, 0)
        inner = adj_ref[t, 3 : 3 + extent, 3 : 3 + extent, :]
        local_ref[t] = masked[t * cells : (t + 1) * cells].reshape(extent, extent, channels) + inner


def scale_of(count):
    return 1.0 / math.sqrt(count * lax.axis_size("lon") * lax.axis_size("lat"))


def run_block(padded, mask, x, saved, g, weights, with_forward, with_backward):
    tiles, side, _, channels = padded.shape
    extent = side - 6
    count = tiles * extent * extent
    hid = weights[4].shape[1]
    operands = [padded, mask]
    operands.append(x if with_forward else saved)
    if with_backward:
        operands.append(g)
    operands.extend(weights)
    shapes = []
    if with_forward:
        shapes += [((count, channels), BF16), ((count, channels), F32)]
    scratch = [pltpu.VMEM((7, tiles, side, extent, channels), F32)]
    if with_backward:
        shapes += [
            ((tiles, extent, extent, channels), F32),
            ((tiles, side, side + 2, channels), F32),
            ((49, channels), F32),
            ((5, channels), F32),
            ((channels, hid), F32),
            ((1, hid), F32),
            ((hid, channels), F32),
        ]
        scratch += [
            pltpu.VMEM((tiles, extent + 12, extent + 16, channels), F32),
            pltpu.VMEM((7, extent + 12, side + 2, channels), F32),
        ]
    vmem = pl.BlockSpec(memory_space=pltpu.VMEM)
    return pl.pallas_call(
        functools.partial(block_kernel, with_forward, with_backward),
        out_shape=tuple(jax.ShapeDtypeStruct(s, d) for s, d in shapes),
        in_specs=[vmem] * len(operands),
        out_specs=tuple([vmem] * len(shapes)),
        scratch_shapes=scratch,
        compiler_params=pltpu.CompilerParams(vmem_limit_bytes=VMEM_LIMIT),
        cost_estimate=pl.CostEstimate(flops=600_000_000, bytes_accessed=6_000_000, transcendentals=400_000),
    )(*operands)


def shards(
    state,
    cotangent,
    land_mask,
    neighbour_codes,
    conv_weight,
    conv_bias,
    normalizer_multiplier,
    norm_bias,
    expand_weight,
    expand_bias,
    project_weight,
    project_bias,
    layer_scale,
):
    slots, channels, cells = state.shape
    extent = math.isqrt(cells)
    layers = conv_weight.shape[0]
    table = link_table(neighbour_codes, slots)
    mask = land_mask.astype(F32).reshape(slots * cells, 1)

    def weights_of(k):
        return [
            conv_weight[k],
            conv_bias[k][None],
            normalizer_multiplier[k][None],
            norm_bias[k][None],
            expand_weight[k],
            expand_bias[k][None],
            project_weight[k],
            project_bias[k][None],
            layer_scale[k][None],
        ]

    grid_shape = (slots, extent, extent, channels)
    x = state.transpose(0, 2, 1).reshape(slots * cells, channels)
    g = cotangent.transpose(0, 2, 1).reshape(slots * cells, channels)
    padded, saved = [], []
    gradients = [None] * layers
    for k in range(layers):
        padded.append(padded_of(x.reshape(grid_shape), table, k))
        last = k == layers - 1
        results = run_block(padded[k], mask, x, None, g if last else None, weights_of(k), True, last)
        x = results[0]
        saved.append(results[1])
    local, adjoint, *gradients[layers - 1] = results[2:]
    for k in reversed(range(layers)):
        if k < layers - 1:
            local, adjoint, *gradients[k] = run_block(
                padded[k], mask, None, saved[k], g, weights_of(k), False, True
            )
        g = gradient_of(local, adjoint, table, layers + k).reshape(slots * cells, channels)
        gradients[k] = lax.psum(tuple(gradients[k]), ("lon", "lat"))

    def outward(values):
        return values.reshape(slots, cells, channels).transpose(0, 2, 1)

    stacked = [jnp.stack([gradients[k][i] for k in range(layers)]) for i in range(5)]
    return (
        outward(x),
        outward(g),
        stacked[0],
        stacked[1],
        stacked[2],
        stacked[3][:, 0],
        stacked[4],
    )


def solution(mesh):
    cells = P(("lon", "lat"), None, None)
    flat = P(("lon", "lat"), None)
    return jax.shard_map(
        shards,
        mesh=mesh,
        in_specs=(cells, cells, flat, flat) + (P(),) * 9,
        out_specs=(cells, cells) + (P(),) * 5,
        check_vma=False,
    )
```

```python
import collections
import functools
import math

import jax
import jax.numpy as jnp
from jax import lax
from jax.experimental import pallas as pl
from jax.experimental.pallas import tpu as pltpu
from jax.sharding import PartitionSpec as P

MESH = pl.DeviceIdType.MESH
GELU_SCALE = 0.7978845608028654
GELU_CUBIC = 0.044715
VMEM_LIMIT = 50 * 1024 * 1024
F32 = jnp.float32
BF16 = jnp.bfloat16
ROWS = 16
LANES = 128


class Exchange:
    def __init__(self, lon_count, lat_count, refs):
        (self.main, self.corner, self.cols, self.got_main, self.got_corner, self.got_cols, self.send_sem, self.recv_sem) = refs
        self.lon_count = lon_count
        self.a = lax.axis_index("lon")
        self.b = lax.axis_index("lat")
        self.top = self.b == lat_count - 1
        self.bottom = self.b == 0
        self.west, self.east = self.wrapped(self.a - 1), self.wrapped(self.a + 1)

    def wrapped(self, i):
        return lax.rem(i + 2 * self.lon_count, self.lon_count)

    def across(self, d):
        return self.wrapped(self.lon_count - 1 - self.a - d)

    def cases(self, d):
        to_self = self.across(d) == self.a
        return (
            jnp.logical_not(self.top),
            jnp.logical_and(self.top, jnp.logical_not(to_self)),
            jnp.logical_and(self.top, to_self),
            jnp.logical_not(self.bottom),
        )

    def greet(self, barrier):
        def hello(lon, lat):
            pl.semaphore_signal(barrier, inc=1, device_id=(lon, lat), device_id_type=MESH)

        hello(self.west, self.b)
        hello(self.east, self.b)
        peers = 2 + jnp.where(self.bottom, 0, 3)
        for d in (-1, 0, 1):
            north, fold, own, south = self.cases(d)
            pl.when(north)(lambda: hello(self.wrapped(self.a + d), self.b + 1))
            pl.when(fold)(lambda: hello(self.across(d), self.b))
            pl.when(south)(lambda: hello(self.wrapped(self.a + d), self.b - 1))
            peers = peers + jnp.where(own, 0, 1)
        return peers

    def source(self, row, d, reverse=False):
        if d == 0:
            return self.main.at[row]
        return self.corner.at[row, 1 if (d > 0) != reverse else 0]

    def landing(self, row, d):
        if d == 0:
            return self.got_main.at[row], row
        return self.got_corner.at[row, 1 if d > 0 else 0], 3 + 2 * row + (1 if d > 0 else 0)

    def message(self, source, landing, number, sending, lon, lat):
        return pltpu.make_async_remote_copy(
            src_ref=source,
            dst_ref=landing,
            send_sem=self.send_sem.at[sending],
            recv_sem=self.recv_sem.at[number],
            device_id=(lon, lat),
            device_id_type=MESH,
        )

    def north(self, d, landing=None):
        target, number = landing or self.landing(1, -d)
        return self.message(self.source(0, d), target, number, 1 + d, self.wrapped(self.a + d), self.b + 1)

    def fold(self, d):
        target, number = self.landing(0, d)
        return self.message(self.source(0, d, True), target, number, 1 + d, self.across(d), self.b)

    def own(self, d):
        target, number = self.landing(0, d)
        return pltpu.make_async_copy(self.source(0, d, True), target, self.recv_sem.at[number])

    def south(self, d, landing=None):
        target, number = landing or self.landing(0, -d)
        return self.message(self.source(1, d), target, number, 4 + d, self.wrapped(self.a + d), self.b - 1)

    def to_west(self):
        return self.message(self.cols.at[0], self.got_cols.at[1], 8, 6, self.west, self.b)

    def to_east(self):
        return self.message(self.cols.at[1], self.got_cols.at[0], 2, 7, self.east, self.b)

    def start(self):
        for d in (0, -1, 1):
            north, fold, own, south = self.cases(d)
            pl.when(fold)(lambda: self.fold(d).start())
            pl.when(own)(lambda: self.own(d).start())
            pl.when(north)(lambda: self.north(d).start())
            pl.when(south)(lambda: self.south(d).start())
        self.to_west().start()
        self.to_east().start()

    def finish(self):
        for d in (0, -1, 1):
            north, fold, own, south = self.cases(d)

            @pl.when(north)
            def _():
                self.north(d).wait_send()
                self.north(d, self.landing(0, d)).wait_recv()

            @pl.when(fold)
            def _():
                self.fold(d).wait_send()
                self.fold(d).wait_recv()

            @pl.when(own)
            def _():
                self.own(d).wait()

            @pl.when(south)
            def _():
                self.south(d).wait_send()
                self.south(d, self.landing(1, d)).wait_recv()

        self.to_west().wait_send()
        self.to_east().wait_send()
        self.to_west().wait_recv()
        self.to_east().wait_recv()


def exchange_kernel(lon_count, lat_count, *refs):
    halo = Exchange(lon_count, lat_count, refs)
    barrier = pltpu.get_barrier_semaphore()
    pl.semaphore_wait(barrier, halo.greet(barrier))
    halo.start()
    halo.finish()


HALO_SEMS = [pltpu.SemaphoreType.DMA((8,)), pltpu.SemaphoreType.DMA((9,))]


def exchange(sent, identity):
    lon_count, lat_count = lax.axis_size("lon"), lax.axis_size("lat")
    vmem = pl.BlockSpec(memory_space=pltpu.VMEM)
    return pl.pallas_call(
        functools.partial(exchange_kernel, lon_count, lat_count),
        out_shape=tuple(jax.ShapeDtypeStruct(x.shape, x.dtype) for x in sent),
        in_specs=[vmem] * 3,
        out_specs=(vmem,) * 3,
        scratch_shapes=HALO_SEMS,
        compiler_params=pltpu.CompilerParams(
            collective_id=identity, has_side_effects=True, vmem_limit_bytes=VMEM_LIMIT
        ),
    )(*sent)


def link_table(codes, slots):
    lon_count, lat_count = lax.axis_size("lon"), lax.axis_size("lat")
    total = slots * lon_count * lat_count
    here = lax.axis_index("lon")
    flipped = codes >= total
    target = jnp.where(flipped, codes - total, codes)
    lon_there = target // slots // lat_count
    centre = jnp.where(flipped, lon_count - 1 - here, here)
    return codes >= 0, lon_there != centre, target % slots


def sent_parts(north, south, west, east):
    slots, _, side, channels = north.shape
    extent = west.shape[1]
    edge = (side - extent) // 2
    top = lax.axis_index("lat") == lax.axis_size("lat") - 1
    strips = jnp.stack([jnp.where(top, jnp.flip(north, (1, 2)), north), south])

    def rows(part):
        return part.reshape(2, slots, -1, channels)

    left, right = rows(strips[:, :, :, :3]), rows(strips[:, :, :, side - 3 :])
    main = rows(strips[:, :, :, edge : side - edge])
    if edge:
        main = jnp.concatenate([main, left, right], axis=2)
        main = jnp.pad(main, ((0, 0), (0, 0), (0, -main.shape[2] % 16), (0, 0)))
    corner = jnp.stack([left, right], axis=1)
    corner = jnp.pad(corner, ((0, 0),) * 3 + ((0, 7), (0, 0)))
    cols = jnp.stack([west.transpose(0, 2, 1, 3), east.transpose(0, 2, 1, 3)])
    return main, corner, cols


def linked_strips(sent, got, table, extent):
    own_cols = sent[2]
    got_main, got_corner, got_cols = got
    valid, away, slot = table
    slots, channels = got_main.shape[1], got_main.shape[3]
    strips = got_main[:, :, : 3 * extent].reshape(2, slots, 3, extent, channels)
    if got_main.shape[2] > 3 * extent:
        low = 3 * extent
        near = [got_main[:, :, low + 9 * i : low + 9 * i + 9] for i in range(2)]
        near = [part.reshape(2, slots, 3, 3, channels) for part in near]
    else:
        near = [strips[:, :, :, :3], strips[:, :, :, extent - 3 :]]
    far = got_corner[:, :, :, :9].reshape(2, 2, slots, 3, 3, channels)

    def pick(near, far, e):
        result = jnp.zeros_like(near)
        for s in range(slots):
            hit = valid[:, e] & (slot[:, e] == s)
            if far is None:
                result = jnp.where(hit[:, None, None, None], near[s][None], result)
            else:
                gone = away[:, e][:, None, None, None]
                result = jnp.where(
                    hit[:, None, None, None], jnp.where(gone, far[s][None], near[s][None]), result
                )
        return result

    north = pick(strips[0], None, 0)
    south = pick(strips[1], None, 1)
    west = pick(own_cols[1], got_cols[0], 2).transpose(0, 2, 1, 3)
    east = pick(own_cols[0], got_cols[1], 3).transpose(0, 2, 1, 3)
    north_west = pick(near[1][0], far[0, 0], 4)
    north_east = pick(near[0][0], far[0, 1], 5)
    south_west = pick(near[1][1], far[1, 0], 6)
    south_east = pick(near[0][1], far[1, 1], 7)
    return north, south, west, east, north_west, north_east, south_west, south_east


def padded_of(x, table, identity):
    extent = x.shape[1]
    sent = sent_parts(x[:, extent - 3 :], x[:, :3], x[:, :, :3], x[:, :, extent - 3 :])
    n, s, w, e, nw, ne, sw, se = linked_strips(sent, exchange(sent, identity), table, extent)
    padded = jnp.concatenate(
        [
            jnp.concatenate([sw, s, se], axis=2),
            jnp.concatenate([w, x, e], axis=2),
            jnp.concatenate([nw, n, ne], axis=2),
        ],
        axis=1,
    )
    return jnp.pad(padded.astype(F32), ((0, 0), (0, 0), (0, 2), (0, 0)))


def frame_parts(adjoint, extent):
    side = extent + 6
    sent = adjoint[:, :, :side].astype(BF16)
    middle = sent[:, 3 : extent + 3]
    return sent_parts(sent[:, side - 3 :], sent[:, :3], middle[:, :, :3], middle[:, :, side - 3 :])


def gradient_of(local, sent, got, table):
    extent = local.shape[1]
    n, s, w, e, nw, ne, sw, se = linked_strips(sent, got, table, extent)
    rest = extent - 3

    def placed(piece, row, col):
        row = (0, rest) if row == 0 else (rest, 0)
        if piece.shape[1] == extent:
            row = (0, 0)
        col = (0, rest) if col == 0 else (rest, 0)
        if piece.shape[2] == extent:
            col = (0, 0)
        return jnp.pad(piece.astype(F32), ((0, 0), row, col, (0, 0)))

    return (
        local
        + placed(n, 1, 0)
        + placed(s, 0, 0)
        + placed(w, 0, 0)
        + placed(e, 0, 1)
        + placed(nw, 1, 0)
        + placed(ne, 1, 1)
        + placed(sw, 0, 0)
        + placed(se, 0, 1)
    ).astype(BF16)


Plan = collections.namedtuple("Plan", ("blocks", "tall", "matrix", "short", "small_blocks", "units"))


def pack_plan(channels, hid):
    blocks, tall = hid // LANES, channels // ROWS
    short = -(-(54 + blocks) // ROWS)
    small_blocks = -(-channels // LANES)
    matrix = blocks * tall
    return Plan(blocks, tall, matrix, short, small_blocks, 2 * matrix + short * small_blocks)


class Sum:
    def __init__(self, lon_count, lat_count, order, pack, result, work, arrived, sems):
        a, b = lax.axis_index("lon"), lax.axis_index("lat")
        self.a, self.b, self.lat_count, self.order = a, b, lat_count, order
        self.core, self.far = lax.rem(a, 2), a // 4
        self.counts = (2, 2 * lat_count, lon_count // 4)
        self.mine = (self.core, lax.rem(a // 2, 2) * lat_count + b, self.far)
        self.pack, self.result, self.work, self.arrived, self.sems = pack, result, work, arrived, sems
        self.base, self.size, self.spans, self.copies = 0, work.shape[0], [], []

    def peer(self, level, j):
        m = lax.rem(self.mine[level] + j, self.counts[level])
        if level == 0:
            return m, (self.a - self.core + m, self.b)
        if level == 1:
            return m, (4 * self.far + 2 * (m // self.lat_count) + self.core, lax.rem(m, self.lat_count))
        return m, (4 * m + lax.rem(self.a, 4), self.b)

    def greet(self, barrier):
        for level in range(3):
            for j in range(1, self.counts[level]):
                pl.semaphore_signal(
                    barrier, inc=1, device_id=self.peer(level, j)[1], device_id_type=MESH
                )
        return sum(self.counts) - 3

    def fill(self):
        low = self.pack.shape[0]
        self.work[:low] = self.pack[...]
        if low < self.work.shape[0]:
            self.work[low:] = jnp.zeros((self.work.shape[0] - low,) + self.work.shape[1:], BF16)

    def start(self, step):
        gather = step >= 3
        level = self.order[5 - step if gather else step]
        if gather:
            base, size = self.spans[5 - step]
        else:
            size = self.size // self.counts[level]
        sems, offset = self.sems[level], 2 if gather else 0
        self.copies = []
        for j in range(1, self.counts[level]):
            m, there = self.peer(level, j)
            if gather:
                source = landing = self.result.at[pl.ds(base, size)]
            else:
                source = self.work.at[pl.ds(self.base + m * size, size)]
                landing = self.arrived[level].at[j - 1]
            copy = pltpu.make_async_remote_copy(
                src_ref=source,
                dst_ref=landing,
                send_sem=sems.at[offset, j - 1],
                recv_sem=sems.at[offset + 1, j - 1],
                device_id=there,
                device_id_type=MESH,
            )
            copy.start()
            self.copies.append(copy)
        if not gather:
            self.size = size
            self.base = self.base + self.mine[level] * size
            self.spans.append((self.base, size))

    def finish(self, step):
        for copy in self.copies:
            copy.wait()
        if step >= 3:
            return
        level = self.order[step]
        span = pl.ds(self.base, self.size)
        total = self.work[span].astype(F32)
        for j in range(1, self.counts[level]):
            total = total + self.arrived[level][j - 1].astype(F32)
        if step < 2:
            self.work[span] = total.astype(BF16)
        else:
            self.result[span] = total.astype(BF16)


ORDERS = ((0, 1, 2), (0, 2, 1))


def reduce_kernel(lon_count, lat_count, parts, *refs):
    packs, halo_in = refs[:parts], refs[parts : parts + 3]
    refs = refs[parts + 3 :]
    results, halo_out = refs[:parts], refs[parts : parts + 3]
    refs = refs[parts + 3 :]
    halo = Exchange(lon_count, lat_count, halo_in + halo_out + refs[:2])
    refs = refs[2:]
    sums = []
    for i in range(parts):
        work, arrived, sems = refs[0], refs[1:4], refs[4:7]
        refs = refs[7:]
        sums.append(
            Sum(lon_count, lat_count, ORDERS[i % 2], packs[i], results[i], work, arrived, sems)
        )
    barrier = pltpu.get_barrier_semaphore()
    peers = halo.greet(barrier) + sums[0].greet(barrier)
    for part in sums:
        part.fill()
    pl.semaphore_wait(barrier, peers)
    halo.start()
    for part in sums:
        part.start(0)
    for step in range(6):
        for part in sums:
            part.finish(step)
            if step < 5:
                part.start(step + 1)
    halo.finish()


def summed(packs, sent, identity):
    lon_count, lat_count = lax.axis_size("lon"), lax.axis_size("lat")
    counts = (2, 2 * lat_count, lon_count // 4)
    devices = lon_count * lat_count
    vmem = pl.BlockSpec(memory_space=pltpu.VMEM)
    scratch, shapes = list(HALO_SEMS), []
    for i, pack in enumerate(packs):
        units = -(-pack.shape[0] // devices) * devices
        shapes.append(jax.ShapeDtypeStruct((units, ROWS, LANES), BF16))
        scratch.append(pltpu.VMEM((units, ROWS, LANES), BF16))
        sizes, size = {}, units
        for level in ORDERS[i % 2]:
            size = size // counts[level]
            sizes[level] = size
        for level in range(3):
            scratch.append(pltpu.VMEM((counts[level] - 1, sizes[level], ROWS, LANES), BF16))
        scratch += [pltpu.SemaphoreType.DMA((4, count - 1)) for count in counts]
    shapes += [jax.ShapeDtypeStruct(x.shape, x.dtype) for x in sent]
    results = pl.pallas_call(
        functools.partial(reduce_kernel, lon_count, lat_count, len(packs)),
        out_shape=tuple(shapes),
        in_specs=[vmem] * (len(packs) + 3),
        out_specs=(vmem,) * len(shapes),
        scratch_shapes=scratch,
        compiler_params=pltpu.CompilerParams(
            collective_id=identity, has_side_effects=True, vmem_limit_bytes=VMEM_LIMIT
        ),
    )(*packs, *sent)
    return results[: len(packs)], results[len(packs) :]


def unpacked(results, channels, hid):
    layers = len(results)
    plan = pack_plan(channels, hid)
    units = jnp.stack([result[: plan.units] for result in results]).astype(F32)
    matrix = (layers, plan.blocks, channels, LANES)
    expand = units[:, : plan.matrix].reshape(matrix).transpose(0, 2, 1, 3)
    project = units[:, plan.matrix : 2 * plan.matrix].reshape(matrix).transpose(0, 1, 3, 2)
    small = units[:, 2 * plan.matrix :].reshape(layers, plan.small_blocks, plan.short * ROWS, LANES)
    rows = small.transpose(0, 2, 1, 3).reshape(layers, plan.short * ROWS, -1)[:, :, :channels]
    return (
        rows[:, :49],
        rows[:, 49:54],
        expand.reshape(layers, channels, hid),
        small[:, 0, 54 : 54 + plan.blocks].reshape(layers, hid),
        project.reshape(layers, hid, channels),
    )


def block_kernel(with_forward, with_backward, padded_ref, mask_ref, *refs):
    refs = list(refs)
    x_ref = refs.pop(0) if with_forward else None
    saved_ref = None if with_forward else refs.pop(0)
    g_ref = refs.pop(0) if with_backward else None
    kernel_ref, cb_ref, gain_ref, shift_ref, we_ref, eb_ref, wp_ref, pb_ref, scale_ref = refs[:9]
    refs = refs[9:]
    out_ref = refs.pop(0) if with_forward else None
    conv_ref = refs.pop(0) if with_forward else saved_ref
    if with_backward:
        local_ref, adj_ref, pack_ref = refs[:3]
        refs = refs[3:]
    shifted = refs.pop(0)
    tiles, padded_side, _, channels = padded_ref.shape
    extent = padded_side - 6
    cells = extent * extent
    count = tiles * cells

    for v in range(7):
        for t in range(tiles):
            shifted[v, t] = padded_ref[t, :, v : v + extent, :]

    if with_forward:
        step = 4
        for t in range(tiles):

            def conv_rows(i, carry, t=t):
                low = i * step
                total = jnp.zeros((step, extent, channels), F32)
                for u in range(7):
                    for v in range(7):
                        total = total + kernel_ref[7 * u + v : 7 * u + v + 1, :][None] * (
                            shifted[v, t, pl.ds(low + u, step)]
                        )
                total = total + cb_ref[...][None]
                start = pl.multiple_of(t * cells + low * extent, step * extent)
                conv_ref[pl.ds(start, step * extent), :] = total.reshape(step * extent, channels)
                return carry

            lax.fori_loop(0, extent // step, conv_rows, 0)

    conv = conv_ref[...]
    centred = conv - jnp.mean(conv, axis=1, keepdims=True)
    inverse = lax.rsqrt(jnp.mean(centred * centred, axis=1, keepdims=True) + 1e-06)
    unit = centred * inverse
    normed = (unit * gain_ref[...] + shift_ref[...]).astype(BF16)
    preact = jnp.dot(normed, we_ref[...], preferred_element_type=F32) + eb_ref[...]
    tangent = jnp.tanh(GELU_SCALE * (preact + GELU_CUBIC * preact * preact * preact))
    hidden = (0.5 * preact * (1.0 + tangent)).astype(BF16)
    branch = jnp.dot(hidden, wp_ref[...], preferred_element_type=F32) + pb_ref[...]
    mask = mask_ref[...]
    if with_forward:
        out_ref[...] = (mask * (x_ref[...].astype(F32) + scale_ref[...] * branch)).astype(BF16)
    if not with_backward:
        return

    grad, low_grad, small = refs
    factor = scale_of(count)
    small[...] = jnp.zeros_like(small)
    masked = mask * g_ref[...].astype(F32)
    branch_grad = scale_ref[...] * masked
    branch_low = branch_grad.astype(BF16)
    hidden_grad = lax.dot_general(
        branch_low, wp_ref[...], (((1,), (1,)), ((), ())), preferred_element_type=F32
    )
    slope = 0.5 * (1.0 + tangent) + 0.5 * preact * (1.0 - tangent * tangent) * GELU_SCALE * (
        1.0 + 3.0 * GELU_CUBIC * preact * preact
    )
    preact_grad = hidden_grad * slope
    preact_low = preact_grad.astype(BF16)
    normed_grad = lax.dot_general(
        preact_low, we_ref[...], (((1,), (1,)), ((), ())), preferred_element_type=F32
    )
    w = normed_grad * gain_ref[...]
    conv_grad = inverse * (
        w
        - jnp.mean(w, axis=1, keepdims=True)
        - unit * jnp.mean(w * unit, axis=1, keepdims=True)
    )

    def row_sum(values):
        return factor * jnp.sum(values, axis=0, keepdims=True)

    small[49:50, 0:channels] = row_sum(conv_grad)
    small[50:51, 0:channels] = row_sum(normed_grad * unit)
    small[51:52, 0:channels] = row_sum(normed_grad)
    small[52:53, 0:channels] = row_sum(branch_grad)
    small[53:54, 0:channels] = row_sum(masked * branch)
    bias_grad = row_sum(preact_grad)
    expand_grad = factor * lax.dot_general(
        normed, preact_low, (((0,), (0,)), ((), ())), preferred_element_type=F32
    )
    project_grad = factor * lax.dot_general(
        branch_low, hidden, (((0,), (0,)), ((), ())), preferred_element_type=F32
    )
    plan = pack_plan(channels, expand_grad.shape[1])
    for i in range(plan.blocks):
        for values, first in ((expand_grad, 0), (project_grad, plan.matrix)):
            low = first + i * plan.tall
            part = values[:, i * LANES : (i + 1) * LANES].astype(BF16)
            pack_ref[low : low + plan.tall] = part.reshape(plan.tall, ROWS, LANES)
        small[54 + i : 55 + i, 0:LANES] = bias_grad[:, i * LANES : (i + 1) * LANES]
    grid = conv_grad.astype(BF16).astype(F32).reshape(tiles, extent, extent, channels)

    grad[...] = jnp.zeros_like(grad)
    for t in range(tiles):
        grad[t, 6 : 6 + extent, 8 : 8 + extent, :] = grid[t]

    for v in range(7):
        sums = tuple(jnp.zeros((extent, channels), F32) for _ in range(7))
        for t in range(tiles):

            def one_row(r, sums, t=t, v=v):
                row = grad[t, 6 + r, 8 : 8 + extent, :]
                return tuple(sums[u] + row * shifted[v, t, r + u] for u in range(7))

            sums = lax.fori_loop(0, extent, one_row, sums)
        for u in range(7):
            small[7 * u + v : 7 * u + v + 1, 0:channels] = row_sum(sums[u])

    for i in range(plan.small_blocks):
        low = 2 * plan.matrix + i * plan.short
        part = small[:, i * LANES : (i + 1) * LANES].astype(BF16)
        pack_ref[low : low + plan.short] = part.reshape(plan.short, ROWS, LANES)

    wide = adj_ref.shape[2]
    for t in range(tiles):
        for v in range(7):
            low_grad[v] = grad[t, :, 8 - v : 8 - v + wide, :]

        def adjoint_rows(i, carry, t=t):
            low = i * 2
            total = jnp.zeros((2, wide, channels), F32)
            for u in range(7):
                for v in range(7):
                    total = total + kernel_ref[7 * u + v : 7 * u + v + 1, :][None] * (
                        low_grad[v, pl.ds(low + 6 - u, 2)]
                    )
            adj_ref[t, pl.ds(low, 2)] = total
            return carry

        lax.fori_loop(0, padded_side // 2, adjoint_rows, 0)
        inner = adj_ref[t, 3 : 3 + extent, 3 : 3 + extent, :]
        local_ref[t] = masked[t * cells : (t + 1) * cells].reshape(extent, extent, channels) + inner


def scale_of(count):
    return 1.0 / math.sqrt(count * lax.axis_size("lon") * lax.axis_size("lat"))


def run_block(padded, mask, x, saved, g, weights, with_forward, with_backward):
    tiles, side, _, channels = padded.shape
    extent = side - 6
    count = tiles * extent * extent
    plan = pack_plan(channels, weights[4].shape[1])
    operands = [padded, mask]
    operands.append(x if with_forward else saved)
    if with_backward:
        operands.append(g)
    operands.extend(weights)
    shapes = []
    if with_forward:
        shapes += [((count, channels), BF16), ((count, channels), F32)]
    scratch = [pltpu.VMEM((7, tiles, side, extent, channels), F32)]
    if with_backward:
        shapes += [
            ((tiles, extent, extent, channels), F32),
            ((tiles, side, side + 2, channels), F32),
            ((plan.units, ROWS, LANES), BF16),
        ]
        scratch += [
            pltpu.VMEM((tiles, extent + 12, extent + 16, channels), F32),
            pltpu.VMEM((7, extent + 12, side + 2, channels), F32),
            pltpu.VMEM((plan.short * ROWS, plan.small_blocks * LANES), F32),
        ]
    vmem = pl.BlockSpec(memory_space=pltpu.VMEM)
    return pl.pallas_call(
        functools.partial(block_kernel, with_forward, with_backward),
        out_shape=tuple(jax.ShapeDtypeStruct(s, d) for s, d in shapes),
        in_specs=[vmem] * len(operands),
        out_specs=tuple([vmem] * len(shapes)),
        scratch_shapes=scratch,
        compiler_params=pltpu.CompilerParams(vmem_limit_bytes=VMEM_LIMIT),
        cost_estimate=pl.CostEstimate(flops=600_000_000, bytes_accessed=6_000_000, transcendentals=400_000),
    )(*operands)


def shards(
    state,
    cotangent,
    land_mask,
    neighbour_codes,
    conv_weight,
    conv_bias,
    normalizer_multiplier,
    norm_bias,
    expand_weight,
    expand_bias,
    project_weight,
    project_bias,
    layer_scale,
):
    slots, channels, cells = state.shape
    extent = math.isqrt(cells)
    layers = conv_weight.shape[0]
    table = link_table(neighbour_codes, slots)
    mask = land_mask.astype(F32).reshape(slots * cells, 1)

    def weights_of(k):
        return [
            conv_weight[k],
            conv_bias[k][None],
            normalizer_multiplier[k][None],
            norm_bias[k][None],
            expand_weight[k],
            expand_bias[k][None],
            project_weight[k],
            project_bias[k][None],
            layer_scale[k][None],
        ]

    grid_shape = (slots, extent, extent, channels)
    x = state.transpose(0, 2, 1).reshape(slots * cells, channels)
    g = cotangent.transpose(0, 2, 1).reshape(slots * cells, channels)
    padded, saved = [], []
    gradients = [None] * layers
    for k in range(layers):
        padded.append(padded_of(x.reshape(grid_shape), table, k))
        last = k == layers - 1
        results = run_block(padded[k], mask, x, None, g if last else None, weights_of(k), True, last)
        x = results[0]
        saved.append(results[1])
    local, adjoint, gradients[layers - 1] = results[2:]
    for k in reversed(range(layers)):
        if k < layers - 1:
            local, adjoint, gradients[k] = run_block(
                padded[k], mask, None, saved[k], g, weights_of(k), False, True
            )
        sent = frame_parts(adjoint, extent)
        if k > 0:
            got = exchange(sent, layers + k)
        else:
            totals, got = summed(gradients, sent, 2 * layers)
        g = gradient_of(local, sent, got, table).reshape(slots * cells, channels)

    def outward(values):
        return values.reshape(slots, cells, channels).transpose(0, 2, 1)

    return (outward(x), outward(g)) + unpacked(totals, channels, expand_weight.shape[2])


def solution(mesh):
    cells = P(("lon", "lat"), None, None)
    flat = P(("lon", "lat"), None)
    return jax.shard_map(
        shards,
        mesh=mesh,
        in_specs=(cells, cells, flat, flat) + (P(),) * 9,
        out_specs=(cells, cells) + (P(),) * 5,
        check_vma=False,
    )
```

```python
import collections
import functools
import math

import jax
import jax.numpy as jnp
from jax import lax
from jax.experimental import pallas as pl
from jax.experimental.pallas import tpu as pltpu
from jax.sharding import PartitionSpec as P

MESH = pl.DeviceIdType.MESH
GELU_SCALE = 0.7978845608028654
GELU_CUBIC = 0.044715
VMEM_LIMIT = 50 * 1024 * 1024
F32 = jnp.float32
BF16 = jnp.bfloat16
ROWS = 16
LANES = 128


class Exchange:
    def __init__(self, lon_count, lat_count, refs):
        (self.main, self.corner, self.cols, self.got_main, self.got_corner, self.got_cols, self.send_sem, self.recv_sem) = refs
        self.lon_count = lon_count
        self.a = lax.axis_index("lon")
        self.b = lax.axis_index("lat")
        self.top = self.b == lat_count - 1
        self.bottom = self.b == 0
        self.west, self.east = self.wrapped(self.a - 1), self.wrapped(self.a + 1)

    def wrapped(self, i):
        return lax.rem(i + 2 * self.lon_count, self.lon_count)

    def across(self, d):
        return self.wrapped(self.lon_count - 1 - self.a - d)

    def cases(self, d):
        to_self = self.across(d) == self.a
        return (
            jnp.logical_not(self.top),
            jnp.logical_and(self.top, jnp.logical_not(to_self)),
            jnp.logical_and(self.top, to_self),
            jnp.logical_not(self.bottom),
        )

    def greet(self, barrier):
        def hello(lon, lat):
            pl.semaphore_signal(barrier, inc=1, device_id=(lon, lat), device_id_type=MESH)

        hello(self.west, self.b)
        hello(self.east, self.b)
        peers = 2 + jnp.where(self.bottom, 0, 3)
        for d in (-1, 0, 1):
            north, fold, own, south = self.cases(d)
            pl.when(north)(lambda: hello(self.wrapped(self.a + d), self.b + 1))
            pl.when(fold)(lambda: hello(self.across(d), self.b))
            pl.when(south)(lambda: hello(self.wrapped(self.a + d), self.b - 1))
            peers = peers + jnp.where(own, 0, 1)
        return peers

    def source(self, row, d, reverse=False):
        if d == 0:
            return self.main.at[row]
        return self.corner.at[row, 1 if (d > 0) != reverse else 0]

    def landing(self, row, d):
        if d == 0:
            return self.got_main.at[row], row
        return self.got_corner.at[row, 1 if d > 0 else 0], 3 + 2 * row + (1 if d > 0 else 0)

    def message(self, source, landing, number, sending, lon, lat):
        return pltpu.make_async_remote_copy(
            src_ref=source,
            dst_ref=landing,
            send_sem=self.send_sem.at[sending],
            recv_sem=self.recv_sem.at[number],
            device_id=(lon, lat),
            device_id_type=MESH,
        )

    def north(self, d, landing=None):
        target, number = landing or self.landing(1, -d)
        return self.message(self.source(0, d), target, number, 1 + d, self.wrapped(self.a + d), self.b + 1)

    def fold(self, d):
        target, number = self.landing(0, d)
        return self.message(self.source(0, d, True), target, number, 1 + d, self.across(d), self.b)

    def own(self, d):
        target, number = self.landing(0, d)
        return pltpu.make_async_copy(self.source(0, d, True), target, self.recv_sem.at[number])

    def south(self, d, landing=None):
        target, number = landing or self.landing(0, -d)
        return self.message(self.source(1, d), target, number, 4 + d, self.wrapped(self.a + d), self.b - 1)

    def to_west(self):
        return self.message(self.cols.at[0], self.got_cols.at[1], 8, 6, self.west, self.b)

    def to_east(self):
        return self.message(self.cols.at[1], self.got_cols.at[0], 2, 7, self.east, self.b)

    def start(self):
        for d in (0, -1, 1):
            north, fold, own, south = self.cases(d)
            pl.when(fold)(lambda: self.fold(d).start())
            pl.when(own)(lambda: self.own(d).start())
            pl.when(north)(lambda: self.north(d).start())
            pl.when(south)(lambda: self.south(d).start())
        self.to_west().start()
        self.to_east().start()

    def finish(self):
        for d in (0, -1, 1):
            north, fold, own, south = self.cases(d)

            @pl.when(north)
            def _():
                self.north(d).wait_send()
                self.north(d, self.landing(0, d)).wait_recv()

            @pl.when(fold)
            def _():
                self.fold(d).wait_send()
                self.fold(d).wait_recv()

            @pl.when(own)
            def _():
                self.own(d).wait()

            @pl.when(south)
            def _():
                self.south(d).wait_send()
                self.south(d, self.landing(1, d)).wait_recv()

        self.to_west().wait_send()
        self.to_east().wait_send()
        self.to_west().wait_recv()
        self.to_east().wait_recv()


def exchange_kernel(lon_count, lat_count, *refs):
    halo = Exchange(lon_count, lat_count, refs)
    barrier = pltpu.get_barrier_semaphore()
    pl.semaphore_wait(barrier, halo.greet(barrier))
    halo.start()
    halo.finish()


HALO_SEMS = [pltpu.SemaphoreType.DMA((8,)), pltpu.SemaphoreType.DMA((9,))]


def exchange(sent, identity):
    lon_count, lat_count = lax.axis_size("lon"), lax.axis_size("lat")
    vmem = pl.BlockSpec(memory_space=pltpu.VMEM)
    return pl.pallas_call(
        functools.partial(exchange_kernel, lon_count, lat_count),
        out_shape=tuple(jax.ShapeDtypeStruct(x.shape, x.dtype) for x in sent),
        in_specs=[vmem] * 3,
        out_specs=(vmem,) * 3,
        scratch_shapes=HALO_SEMS,
        compiler_params=pltpu.CompilerParams(
            collective_id=identity, has_side_effects=True, vmem_limit_bytes=VMEM_LIMIT
        ),
    )(*sent)


def link_table(codes, slots):
    lon_count, lat_count = lax.axis_size("lon"), lax.axis_size("lat")
    total = slots * lon_count * lat_count
    here = lax.axis_index("lon")
    flipped = codes >= total
    target = jnp.where(flipped, codes - total, codes)
    lon_there = target // slots // lat_count
    centre = jnp.where(flipped, lon_count - 1 - here, here)
    return codes >= 0, lon_there != centre, target % slots


def sent_parts(north, south, west, east):
    slots, _, side, channels = north.shape
    extent = west.shape[1]
    edge = (side - extent) // 2
    top = lax.axis_index("lat") == lax.axis_size("lat") - 1
    strips = jnp.stack([jnp.where(top, jnp.flip(north, (1, 2)), north), south])

    def rows(part):
        return part.reshape(2, slots, -1, channels)

    left, right = rows(strips[:, :, :, :3]), rows(strips[:, :, :, side - 3 :])
    main = rows(strips[:, :, :, edge : side - edge])
    if edge:
        main = jnp.concatenate([main, left, right], axis=2)
        main = jnp.pad(main, ((0, 0), (0, 0), (0, -main.shape[2] % 16), (0, 0)))
    corner = jnp.stack([left, right], axis=1)
    corner = jnp.pad(corner, ((0, 0),) * 3 + ((0, 7), (0, 0)))
    cols = jnp.stack([west.transpose(0, 2, 1, 3), east.transpose(0, 2, 1, 3)])
    return main, corner, cols


def linked_strips(sent, got, table, extent):
    own_cols = sent[2]
    got_main, got_corner, got_cols = got
    valid, away, slot = table
    slots, channels = got_main.shape[1], got_main.shape[3]
    strips = got_main[:, :, : 3 * extent].reshape(2, slots, 3, extent, channels)
    if got_main.shape[2] > 3 * extent:
        low = 3 * extent
        near = [got_main[:, :, low + 9 * i : low + 9 * i + 9] for i in range(2)]
        near = [part.reshape(2, slots, 3, 3, channels) for part in near]
    else:
        near = [strips[:, :, :, :3], strips[:, :, :, extent - 3 :]]
    far = got_corner[:, :, :, :9].reshape(2, 2, slots, 3, 3, channels)

    def pick(near, far, e):
        result = jnp.zeros_like(near)
        for s in range(slots):
            hit = valid[:, e] & (slot[:, e] == s)
            if far is None:
                result = jnp.where(hit[:, None, None, None], near[s][None], result)
            else:
                gone = away[:, e][:, None, None, None]
                result = jnp.where(
                    hit[:, None, None, None], jnp.where(gone, far[s][None], near[s][None]), result
                )
        return result

    north = pick(strips[0], None, 0)
    south = pick(strips[1], None, 1)
    west = pick(own_cols[1], got_cols[0], 2).transpose(0, 2, 1, 3)
    east = pick(own_cols[0], got_cols[1], 3).transpose(0, 2, 1, 3)
    north_west = pick(near[1][0], far[0, 0], 4)
    north_east = pick(near[0][0], far[0, 1], 5)
    south_west = pick(near[1][1], far[1, 0], 6)
    south_east = pick(near[0][1], far[1, 1], 7)
    return north, south, west, east, north_west, north_east, south_west, south_east


def padded_of(x, table, identity):
    extent = x.shape[1]
    sent = sent_parts(x[:, extent - 3 :], x[:, :3], x[:, :, :3], x[:, :, extent - 3 :])
    n, s, w, e, nw, ne, sw, se = linked_strips(sent, exchange(sent, identity), table, extent)
    padded = jnp.concatenate(
        [
            jnp.concatenate([sw, s, se], axis=2),
            jnp.concatenate([w, x, e], axis=2),
            jnp.concatenate([nw, n, ne], axis=2),
        ],
        axis=1,
    )
    return jnp.pad(padded.astype(F32), ((0, 0), (0, 0), (0, 2), (0, 0)))


def frame_parts(adjoint, extent):
    side = extent + 6
    sent = adjoint[:, :, :side].astype(BF16)
    middle = sent[:, 3 : extent + 3]
    return sent_parts(sent[:, side - 3 :], sent[:, :3], middle[:, :, :3], middle[:, :, side - 3 :])


def gradient_of(local, sent, got, table):
    extent = local.shape[1]
    n, s, w, e, nw, ne, sw, se = linked_strips(sent, got, table, extent)
    rest = extent - 3

    def placed(piece, row, col):
        row = (0, rest) if row == 0 else (rest, 0)
        if piece.shape[1] == extent:
            row = (0, 0)
        col = (0, rest) if col == 0 else (rest, 0)
        if piece.shape[2] == extent:
            col = (0, 0)
        return jnp.pad(piece.astype(F32), ((0, 0), row, col, (0, 0)))

    return (
        local
        + placed(n, 1, 0)
        + placed(s, 0, 0)
        + placed(w, 0, 0)
        + placed(e, 0, 1)
        + placed(nw, 1, 0)
        + placed(ne, 1, 1)
        + placed(sw, 0, 0)
        + placed(se, 0, 1)
    ).astype(BF16)


Plan = collections.namedtuple("Plan", ("blocks", "tall", "matrix", "short", "small_blocks", "units"))


def pack_plan(channels, hid):
    blocks, tall = hid // LANES, channels // ROWS
    short = -(-(54 + blocks) // ROWS)
    small_blocks = -(-channels // LANES)
    matrix = blocks * tall
    return Plan(blocks, tall, matrix, short, small_blocks, 2 * matrix + short * small_blocks)


class Sum:
    def __init__(self, lon_count, lat_count, order, pack, result, work, arrived, sems):
        a, b = lax.axis_index("lon"), lax.axis_index("lat")
        self.a, self.b, self.lat_count, self.order = a, b, lat_count, order
        self.core, self.far = lax.rem(a, 2), a // 4
        self.counts = (2, 2 * lat_count, lon_count // 4)
        self.mine = (self.core, lax.rem(a // 2, 2) * lat_count + b, self.far)
        self.pack, self.result, self.work, self.arrived, self.sems = pack, result, work, arrived, sems
        self.base, self.size, self.spans, self.copies = 0, work.shape[0], [], []

    def peer(self, level, j):
        m = lax.rem(self.mine[level] + j, self.counts[level])
        if level == 0:
            return m, (self.a - self.core + m, self.b)
        if level == 1:
            return m, (4 * self.far + 2 * (m // self.lat_count) + self.core, lax.rem(m, self.lat_count))
        return m, (4 * m + lax.rem(self.a, 4), self.b)

    def greet(self, barrier):
        for level in range(3):
            for j in range(1, self.counts[level]):
                pl.semaphore_signal(
                    barrier, inc=1, device_id=self.peer(level, j)[1], device_id_type=MESH
                )
        return sum(self.counts) - 3

    def fill(self):
        low = self.pack.shape[0]
        self.work[:low] = self.pack[...]
        if low < self.work.shape[0]:
            self.work[low:] = jnp.zeros((self.work.shape[0] - low,) + self.work.shape[1:], BF16)

    def start(self, step):
        gather = step >= 3
        level = self.order[5 - step if gather else step]
        if gather:
            base, size = self.spans[5 - step]
        else:
            size = self.size // self.counts[level]
        sems, offset = self.sems[level], 2 if gather else 0
        self.copies = []
        for j in range(1, self.counts[level]):
            m, there = self.peer(level, j)
            if gather:
                source = landing = self.result.at[pl.ds(base, size)]
            else:
                source = self.work.at[pl.ds(self.base + m * size, size)]
                landing = self.arrived[level].at[j - 1]
            copy = pltpu.make_async_remote_copy(
                src_ref=source,
                dst_ref=landing,
                send_sem=sems.at[offset, j - 1],
                recv_sem=sems.at[offset + 1, j - 1],
                device_id=there,
                device_id_type=MESH,
            )
            copy.start()
            self.copies.append(copy)
        if not gather:
            self.size = size
            self.base = self.base + self.mine[level] * size
            self.spans.append((self.base, size))

    def finish(self, step):
        for copy in self.copies:
            copy.wait()
        if step >= 3:
            return
        level = self.order[step]
        span = pl.ds(self.base, self.size)
        total = self.work[span].astype(F32)
        for j in range(1, self.counts[level]):
            total = total + self.arrived[level][j - 1].astype(F32)
        if step < 2:
            self.work[span] = total.astype(BF16)
        else:
            self.result[span] = total.astype(BF16)


ORDERS = ((0, 1, 2), (0, 2, 1))


def reduce_kernel(lon_count, lat_count, parts, *refs):
    packs, halo_in = refs[:parts], refs[parts : parts + 3]
    refs = refs[parts + 3 :]
    results, halo_out = refs[:parts], refs[parts : parts + 3]
    refs = refs[parts + 3 :]
    halo = Exchange(lon_count, lat_count, halo_in + halo_out + refs[:2])
    refs = refs[2:]
    sums = []
    for i in range(parts):
        work, arrived, sems = refs[0], refs[1:4], refs[4:7]
        refs = refs[7:]
        sums.append(
            Sum(lon_count, lat_count, ORDERS[i % 2], packs[i], results[i], work, arrived, sems)
        )
    barrier = pltpu.get_barrier_semaphore()
    peers = halo.greet(barrier) + sums[0].greet(barrier)
    for part in sums:
        part.fill()
    pl.semaphore_wait(barrier, peers)
    halo.start()
    for part in sums:
        part.start(0)
    for step in range(6):
        for part in sums:
            part.finish(step)
            if step < 5:
                part.start(step + 1)
    halo.finish()


def summed(packs, sent, identity):
    lon_count, lat_count = lax.axis_size("lon"), lax.axis_size("lat")
    counts = (2, 2 * lat_count, lon_count // 4)
    devices = lon_count * lat_count
    vmem = pl.BlockSpec(memory_space=pltpu.VMEM)
    scratch, shapes = list(HALO_SEMS), []
    for i, pack in enumerate(packs):
        units = -(-pack.shape[0] // devices) * devices
        shapes.append(jax.ShapeDtypeStruct((units, ROWS, LANES), BF16))
        scratch.append(pltpu.VMEM((units, ROWS, LANES), BF16))
        sizes, size = {}, units
        for level in ORDERS[i % 2]:
            size = size // counts[level]
            sizes[level] = size
        for level in range(3):
            scratch.append(pltpu.VMEM((counts[level] - 1, sizes[level], ROWS, LANES), BF16))
        scratch += [pltpu.SemaphoreType.DMA((4, count - 1)) for count in counts]
    shapes += [jax.ShapeDtypeStruct(x.shape, x.dtype) for x in sent]
    results = pl.pallas_call(
        functools.partial(reduce_kernel, lon_count, lat_count, len(packs)),
        out_shape=tuple(shapes),
        in_specs=[vmem] * (len(packs) + 3),
        out_specs=(vmem,) * len(shapes),
        scratch_shapes=scratch,
        compiler_params=pltpu.CompilerParams(
            collective_id=identity, has_side_effects=True, vmem_limit_bytes=VMEM_LIMIT
        ),
    )(*packs, *sent)
    return results[: len(packs)], results[len(packs) :]


def unpacked(results, channels, hid):
    layers = len(results)
    plan = pack_plan(channels, hid)
    units = jnp.stack([result[: plan.units] for result in results]).astype(F32)
    matrix = (layers, plan.blocks, channels, LANES)
    expand = units[:, : plan.matrix].reshape(matrix).transpose(0, 2, 1, 3)
    project = units[:, plan.matrix : 2 * plan.matrix].reshape(matrix).transpose(0, 1, 3, 2)
    small = units[:, 2 * plan.matrix :].reshape(layers, plan.small_blocks, plan.short * ROWS, LANES)
    rows = small.transpose(0, 2, 1, 3).reshape(layers, plan.short * ROWS, -1)[:, :, :channels]
    return (
        rows[:, :49],
        rows[:, 49:54],
        expand.reshape(layers, channels, hid),
        small[:, 0, 54 : 54 + plan.blocks].reshape(layers, hid),
        project.reshape(layers, hid, channels),
    )


def block_kernel(layer, with_forward, with_backward, padded_ref, mask_ref, *refs):
    refs = list(refs)
    x_ref = refs.pop(0) if with_forward else None
    saved_ref = None if with_forward else refs.pop(0)
    g_ref = refs.pop(0) if with_backward else None
    weights = [ref.at[layer] if len(ref.shape) == 3 else ref.at[layer : layer + 1] for ref in refs[:9]]
    kernel_ref, cb_ref, gain_ref, shift_ref, we_ref, eb_ref, wp_ref, pb_ref, scale_ref = weights
    refs = refs[9:]
    out_ref = refs.pop(0) if with_forward else None
    conv_ref = refs.pop(0) if with_forward else saved_ref
    if with_backward:
        local_ref, adj_ref, pack_ref = refs[:3]
        refs = refs[3:]
    shifted = refs.pop(0)
    tiles, padded_side, _, channels = padded_ref.shape
    extent = padded_side - 6
    cells = extent * extent
    count = tiles * cells

    for v in range(7):
        for t in range(tiles):
            shifted[v, t] = padded_ref[t, :, v : v + extent, :]

    if with_forward:
        step = 4
        for t in range(tiles):

            def conv_rows(i, carry, t=t):
                low = i * step
                total = jnp.zeros((step, extent, channels), F32)
                for u in range(7):
                    for v in range(7):
                        total = total + kernel_ref[7 * u + v : 7 * u + v + 1, :][None] * (
                            shifted[v, t, pl.ds(low + u, step)]
                        )
                total = total + cb_ref[...][None]
                start = pl.multiple_of(t * cells + low * extent, step * extent)
                conv_ref[pl.ds(start, step * extent), :] = total.reshape(step * extent, channels)
                return carry

            lax.fori_loop(0, extent // step, conv_rows, 0)

    conv = conv_ref[...]
    centred = conv - jnp.mean(conv, axis=1, keepdims=True)
    inverse = lax.rsqrt(jnp.mean(centred * centred, axis=1, keepdims=True) + 1e-06)
    unit = centred * inverse
    normed = (unit * gain_ref[...] + shift_ref[...]).astype(BF16)
    preact = jnp.dot(normed, we_ref[...], preferred_element_type=F32) + eb_ref[...]
    tangent = jnp.tanh(GELU_SCALE * (preact + GELU_CUBIC * preact * preact * preact))
    hidden = (0.5 * preact * (1.0 + tangent)).astype(BF16)
    branch = jnp.dot(hidden, wp_ref[...], preferred_element_type=F32) + pb_ref[...]
    mask = mask_ref[...]
    if with_forward:
        out_ref[...] = (mask * (x_ref[...].astype(F32) + scale_ref[...] * branch)).astype(BF16)
    if not with_backward:
        return

    grad, low_grad, small = refs
    factor = scale_of(count)
    small[...] = jnp.zeros_like(small)
    masked = mask * g_ref[...].astype(F32)
    branch_grad = scale_ref[...] * masked
    branch_low = branch_grad.astype(BF16)
    hidden_grad = lax.dot_general(
        branch_low, wp_ref[...], (((1,), (1,)), ((), ())), preferred_element_type=F32
    )
    slope = 0.5 * (1.0 + tangent) + 0.5 * preact * (1.0 - tangent * tangent) * GELU_SCALE * (
        1.0 + 3.0 * GELU_CUBIC * preact * preact
    )
    preact_grad = hidden_grad * slope
    preact_low = preact_grad.astype(BF16)
    normed_grad = lax.dot_general(
        preact_low, we_ref[...], (((1,), (1,)), ((), ())), preferred_element_type=F32
    )
    w = normed_grad * gain_ref[...]
    conv_grad = inverse * (
        w
        - jnp.mean(w, axis=1, keepdims=True)
        - unit * jnp.mean(w * unit, axis=1, keepdims=True)
    )

    def row_sum(values):
        return factor * jnp.sum(values, axis=0, keepdims=True)

    small[49:50, 0:channels] = row_sum(conv_grad)
    small[50:51, 0:channels] = row_sum(normed_grad * unit)
    small[51:52, 0:channels] = row_sum(normed_grad)
    small[52:53, 0:channels] = row_sum(branch_grad)
    small[53:54, 0:channels] = row_sum(masked * branch)
    bias_grad = row_sum(preact_grad)
    expand_grad = factor * lax.dot_general(
        normed, preact_low, (((0,), (0,)), ((), ())), preferred_element_type=F32
    )
    project_grad = factor * lax.dot_general(
        branch_low, hidden, (((0,), (0,)), ((), ())), preferred_element_type=F32
    )
    plan = pack_plan(channels, expand_grad.shape[1])
    for i in range(plan.blocks):
        for values, first in ((expand_grad, 0), (project_grad, plan.matrix)):
            low = first + i * plan.tall
            part = values[:, i * LANES : (i + 1) * LANES].astype(BF16)
            pack_ref[low : low + plan.tall] = part.reshape(plan.tall, ROWS, LANES)
        small[54 + i : 55 + i, 0:LANES] = bias_grad[:, i * LANES : (i + 1) * LANES]
    grid = conv_grad.astype(BF16).astype(F32).reshape(tiles, extent, extent, channels)

    grad[...] = jnp.zeros_like(grad)
    for t in range(tiles):
        grad[t, 6 : 6 + extent, 8 : 8 + extent, :] = grid[t]

    for v in range(7):
        sums = tuple(jnp.zeros((extent, channels), F32) for _ in range(7))
        for t in range(tiles):

            def one_row(r, sums, t=t, v=v):
                row = grad[t, 6 + r, 8 : 8 + extent, :]
                return tuple(sums[u] + row * shifted[v, t, r + u] for u in range(7))

            sums = lax.fori_loop(0, extent, one_row, sums)
        for u in range(7):
            small[7 * u + v : 7 * u + v + 1, 0:channels] = row_sum(sums[u])

    for i in range(plan.small_blocks):
        low = 2 * plan.matrix + i * plan.short
        part = small[:, i * LANES : (i + 1) * LANES].astype(BF16)
        pack_ref[low : low + plan.short] = part.reshape(plan.short, ROWS, LANES)

    wide = adj_ref.shape[2]
    for t in range(tiles):
        for v in range(7):
            low_grad[v] = grad[t, :, 8 - v : 8 - v + wide, :]

        def adjoint_rows(i, carry, t=t):
            low = i * 2
            total = jnp.zeros((2, wide, channels), F32)
            for u in range(7):
                for v in range(7):
                    total = total + kernel_ref[7 * u + v : 7 * u + v + 1, :][None] * (
                        low_grad[v, pl.ds(low + 6 - u, 2)]
                    )
            adj_ref[t, pl.ds(low, 2)] = total
            return carry

        lax.fori_loop(0, padded_side // 2, adjoint_rows, 0)
        inner = adj_ref[t, 3 : 3 + extent, 3 : 3 + extent, :]
        local_ref[t] = masked[t * cells : (t + 1) * cells].reshape(extent, extent, channels) + inner


def scale_of(count):
    return 1.0 / math.sqrt(count * lax.axis_size("lon") * lax.axis_size("lat"))


def run_block(layer, padded, mask, x, saved, g, weights, with_forward, with_backward):
    tiles, side, _, channels = padded.shape
    extent = side - 6
    count = tiles * extent * extent
    plan = pack_plan(channels, weights[4].shape[2])
    operands = [padded, mask]
    operands.append(x if with_forward else saved)
    if with_backward:
        operands.append(g)
    operands.extend(weights)
    shapes = []
    if with_forward:
        shapes += [((count, channels), BF16), ((count, channels), F32)]
    scratch = [pltpu.VMEM((7, tiles, side, extent, channels), F32)]
    if with_backward:
        shapes += [
            ((tiles, extent, extent, channels), F32),
            ((tiles, side, side + 2, channels), F32),
            ((plan.units, ROWS, LANES), BF16),
        ]
        scratch += [
            pltpu.VMEM((tiles, extent + 12, extent + 16, channels), F32),
            pltpu.VMEM((7, extent + 12, side + 2, channels), F32),
            pltpu.VMEM((plan.short * ROWS, plan.small_blocks * LANES), F32),
        ]
    vmem = pl.BlockSpec(memory_space=pltpu.VMEM)
    return pl.pallas_call(
        functools.partial(block_kernel, layer, with_forward, with_backward),
        out_shape=tuple(jax.ShapeDtypeStruct(s, d) for s, d in shapes),
        in_specs=[vmem] * len(operands),
        out_specs=tuple([vmem] * len(shapes)),
        scratch_shapes=scratch,
        compiler_params=pltpu.CompilerParams(vmem_limit_bytes=VMEM_LIMIT),
        cost_estimate=pl.CostEstimate(flops=600_000_000, bytes_accessed=6_000_000, transcendentals=400_000),
    )(*operands)


def shards(
    state,
    cotangent,
    land_mask,
    neighbour_codes,
    conv_weight,
    conv_bias,
    normalizer_multiplier,
    norm_bias,
    expand_weight,
    expand_bias,
    project_weight,
    project_bias,
    layer_scale,
):
    slots, channels, cells = state.shape
    extent = math.isqrt(cells)
    layers = conv_weight.shape[0]
    table = link_table(neighbour_codes, slots)
    mask = land_mask.astype(F32).reshape(slots * cells, 1)

    weights = [
        conv_weight,
        conv_bias,
        normalizer_multiplier,
        norm_bias,
        expand_weight,
        expand_bias,
        project_weight,
        project_bias,
        layer_scale,
    ]
    grid_shape = (slots, extent, extent, channels)
    x = state.transpose(0, 2, 1).reshape(slots * cells, channels)
    g = cotangent.transpose(0, 2, 1).reshape(slots * cells, channels)
    padded, saved = [], []
    gradients = [None] * layers
    for k in range(layers):
        padded.append(padded_of(x.reshape(grid_shape), table, k))
        last = k == layers - 1
        results = run_block(k, padded[k], mask, x, None, g if last else None, weights, True, last)
        x = results[0]
        saved.append(results[1])
    local, adjoint, gradients[layers - 1] = results[2:]
    for k in reversed(range(layers)):
        if k < layers - 1:
            local, adjoint, gradients[k] = run_block(
                k, padded[k], mask, None, saved[k], g, weights, False, True
            )
        sent = frame_parts(adjoint, extent)
        if k > 0:
            got = exchange(sent, layers + k)
        else:
            totals, got = summed(gradients, sent, 2 * layers)
        g = gradient_of(local, sent, got, table).reshape(slots * cells, channels)

    def outward(values):
        return values.reshape(slots, cells, channels).transpose(0, 2, 1)

    return (outward(x), outward(g)) + unpacked(totals, channels, expand_weight.shape[2])


def solution(mesh):
    cells = P(("lon", "lat"), None, None)
    flat = P(("lon", "lat"), None)
    return jax.shard_map(
        shards,
        mesh=mesh,
        in_specs=(cells, cells, flat, flat) + (P(),) * 9,
        out_specs=(cells, cells) + (P(),) * 5,
        check_vma=False,
    )
```
